32 devices in a mesh: section: 2 (over core), expert: 8 (over z, x), dp: 2 (over y).
Axes of the slice: x: 2, y: 2, z: 4, core: 2. Of those that a mesh axis runs over, the one named last changes fastest.
Arguments:
- layer_inputs: bfloat16 [2, 1024, 2048], P('section', 'expert'), may hold values from -6 to 6
- out_grad: bfloat16 [1024, 2048], P('expert'), may hold values from -6 to 6
- expert_ids: int32 [2, 1024, 6], P('section', 'expert'), may hold values from 0 to 15, all different within a row; in each aligned block of 128 rows (0 to 127, 128 to 255, ..., all dimensions but the last counted through in order) at most 64 rows name the same one
- gate_weights: float32 [2, 1024, 6], P('section', 'expert'), may hold values from 0.05 to 0.5
- w_gate: bfloat16 [2, 16, 2048, 1408], P('section', 'expert', None, 'dp'), may hold values from -0.125 to 0.125
- w_up: bfloat16 [2, 16, 2048, 1408], P('section', 'expert', None, 'dp'), may hold values from -0.125 to 0.125
- w_down: bfloat16 [2, 16, 1408, 2048], P('section', 'expert', 'dp'), may hold values from -0.15625 to 0.15625
Outputs:
- input_grads: bfloat16 [2, 1024, 2048], P('section', 'expert')
The draws below stay inside these ranges and needn't reach their ends.
Inputs may be any that keep to these rules, and one draw needn't show every extreme that they name: `expert_ids`: each row names 6 different experts. In the 128 rows of one index of expert, no expert of a layer is named by more than 64 rows, a bound that some block reaches.
All inputs are finite; a program needn't handle non-finite values.
Results may differ from the reference program's by a relative error of at most 0.006.
Values may be sent and summed in bfloat16 or wider, within the bound.
No kernel may reach another device: no remote copies, remote signals or barrier semaphores. Data moves between devices by JAX's collectives and lax.ppermute only.
A program may use at most 128 MiB of HBM per device.

```python
import math
import jax
import jax.numpy as jnp
import numpy as np
from jax import lax

D = 2048
FF = 1408
TOP = 6
TOK_DEV = 128
EXPERTS = 16
LAYERS = 2
TOKENS = 1024
CAP = 64
N_EXPERT = 8
N_DP = 2


def levels(rng, shape, shards, smallest, high):
    def one(dim, parts):
        draws = jax.random.uniform(jax.random.fold_in(jax.random.fold_in(rng, 6), dim), (parts,), jnp.float32, smallest / len(shards), high / len(shards))
        return jnp.repeat(jnp.exp(draws), shape[dim] // parts).reshape((-1,) + (1,) * (len(shape) - dim - 1))

    level = one(*shards[0])
    for cut in shards[1:]:
        level = level * one(*cut)
    return level


def assign_block(stream_key, own, number, rows, amount, top, limit, skew):
    order = jax.random.permutation(stream_key, amount)
    crowded, common = portions_of(amount, rows * top, limit, skew, True), portions_of(amount, rows * top, limit, skew, False)
    places = jnp.arange(amount)

    def named(sizes, turn):
        used = int((sizes > 0).sum())
        fixed = max(1, used // 4)
        moved = fixed + (places - fixed + turn * (used - fixed)) % max(1, amount - fixed)
        return jnp.zeros((amount,), jnp.int32).at[order[jnp.where(places < fixed, places, moved)]].set(jnp.asarray(sizes, jnp.int32))

    sizes = jnp.where(number % 4 == 0, named(crowded, number // 4), named(common, number - number // 4 - 1))
    mixed = jax.random.permutation(jax.random.fold_in(own, 3), amount)
    donor, receiver = mixed[0:amount // 2 * 2:2], mixed[1:amount // 2 * 2:2]
    room = jnp.minimum(sizes[donor] - 1, limit - sizes[receiver]) // 2
    room = jnp.where((donor == order[0]) | (receiver == order[0]) | (sizes[receiver] == 0), 0, jnp.maximum(room, 0))
    moved = jax.random.randint(jax.random.fold_in(own, 4), (amount // 2,), 0, 1 << 20) % (room + 1)
    sizes = sizes.at[donor].add(-moved).at[receiver].add(moved)
    members = jnp.searchsorted(jnp.cumsum(sizes), jnp.arange(rows * top), side="right").astype(jnp.int32)
    listing = members.reshape(top, rows).T
    listing = listing[jax.random.permutation(jax.random.fold_in(own, 1), rows)]
    turn = jax.random.randint(jax.random.fold_in(own, 2), (rows, 1), 0, top)
    return jnp.take_along_axis(listing, (jnp.arange(top)[None, :] + turn) % top, axis=1)


def portions_of(number_of, total, reach, lean, full):
    loads = [(1 << 20) // math.isqrt(grade ** lean) + 1 for grade in range(1, number_of + 1)]
    largest = reach if full else min(reach, max(-(-total // number_of), total * loads[0] // sum(loads)))
    least = 1 if total - largest >= number_of - 1 else 0
    given, rest = [largest] + [least] * (number_of - 1), total - largest - least * (number_of - 1)
    while rest > 0:
        candidates = [i for i in range(1, number_of) if given[i] < largest] or [i for i in range(1, number_of) if given[i] < reach]
        pool, budget = sum([loads[i] for i in candidates]), rest
        for i in candidates:
            addition = min(reach - given[i], max(1, budget * loads[i] // pool), rest)
            given[i] = given[i] + addition
            rest = rest - addition
    return np.array(given)


def scatter_about(rng, extent, width, limit, shards=(), held_as=jnp.bfloat16):
    factor_of = levels(rng, extent, shards, -0.22, 0.18) if shards else 1.0
    values = jax.random.normal(rng, extent, jnp.float32) * width * factor_of
    return jnp.minimum(jnp.maximum(values, -limit), limit).astype(held_as)


def setup_inputs(seed: int = 0) -> dict:
    seeds = jax.random.split(jax.random.key(seed), 8)
    layer_inputs = scatter_about(seeds[0], (LAYERS, TOKENS, D), 1.0, 6.0, ((0, 2), (1, 8)))
    out_grad = scatter_about(seeds[1], (TOKENS, D), 1.0, 6.0, ((0, 8),))
    expert_ids_keys = jax.random.split(jax.random.fold_in(seeds[2], 1), LAYERS * TOKENS // TOK_DEV)
    expert_ids_turns = jax.random.permutation(jax.random.fold_in(seeds[2], 3), LAYERS * TOKENS // TOK_DEV)
    expert_ids = jax.vmap(lambda own, number: assign_block(jax.random.fold_in(seeds[2], 2), own, number, TOK_DEV, EXPERTS, TOP, CAP, 1))(expert_ids_keys, expert_ids_turns).reshape((LAYERS, TOKENS, TOP))
    gate_weights = jnp.clip(0.05 + 0.45 * jax.random.uniform(seeds[3], (LAYERS, TOKENS, TOP), jnp.float32) ** levels(seeds[3], (LAYERS, TOKENS, TOP), ((0, 2), (1, 8)), -0.2, 0.2), 0.05, 0.5)
    w_gate = scatter_about(seeds[4], (LAYERS, EXPERTS, D, FF), D ** -0.5, 0.125, ((0, 2), (1, 8), (3, 2)))
    w_up = scatter_about(seeds[5], (LAYERS, EXPERTS, D, FF), D ** -0.5, 0.125, ((0, 2), (1, 8), (3, 2)))
    w_down = scatter_about(seeds[6], (LAYERS, EXPERTS, FF, D), FF ** -0.5, 0.15625, ((0, 2), (1, 8), (2, 2)))
    return dict(layer_inputs=layer_inputs, out_grad=out_grad, expert_ids=expert_ids, gate_weights=gate_weights, w_gate=w_gate, w_up=w_up, w_down=w_down)


def expert_rows(table_row, gate_mat, up_mat, down_mat, input_pad, cot_pad):
    highest = lax.Precision.HIGHEST
    in_rows = jnp.take(input_pad, table_row, axis=0).astype(jnp.float32)
    cot_rows = jnp.take(cot_pad, table_row, axis=0).astype(jnp.float32)
    gate_f32 = gate_mat.astype(jnp.float32)
    up_f32 = up_mat.astype(jnp.float32)
    down_f32 = down_mat.astype(jnp.float32)
    pre_gate = jnp.dot(in_rows, gate_f32, precision=highest)
    pre_up = jnp.dot(in_rows, up_f32, precision=highest)
    hidden_grad = jnp.dot(cot_rows, down_f32.T, precision=highest)
    sig_value = jax.nn.sigmoid(pre_gate)
    gate_grad = (hidden_grad * pre_up * sig_value * (1.0 + pre_gate * (1.0 - sig_value))).astype(jnp.bfloat16)
    up_grad = (hidden_grad * pre_gate * sig_value).astype(jnp.bfloat16)
    gate_grad = lax.optimization_barrier(gate_grad).astype(jnp.float32)
    up_grad = lax.optimization_barrier(up_grad).astype(jnp.float32)
    row_count = in_rows.shape[0]
    block_width = FF // N_DP
    gate_blocks = gate_grad.reshape(row_count, N_DP, block_width)
    up_blocks = up_grad.reshape(row_count, N_DP, block_width)
    gate_wblk = gate_f32.reshape(D, N_DP, block_width)
    up_wblk = up_f32.reshape(D, N_DP, block_width)
    partial_value = jnp.einsum('mqf,dqf->qmd', gate_blocks, gate_wblk, precision=highest)
    partial_value = partial_value + jnp.einsum('mqf,dqf->qmd', up_blocks, up_wblk, precision=highest)
    partial_value = lax.optimization_barrier(partial_value.astype(jnp.bfloat16))
    return lax.optimization_barrier(jnp.sum(partial_value.astype(jnp.float32), axis=0))

def layer_grad(inputs, cotangent, route_ids, gate_vals, w_gate, w_up, w_down):
    token_total = inputs.shape[0]
    blocks = route_ids.reshape(N_EXPERT, TOK_DEV * TOP)
    hit_table = (blocks[:, :, None] == jnp.arange(EXPERTS, dtype=jnp.int32)[None, None, :]).astype(jnp.int32)
    position = lax.optimization_barrier(jnp.sum((jnp.cumsum(hit_table, axis=1) - hit_table) * hit_table, axis=2))
    source_block = jnp.arange(N_EXPERT, dtype=jnp.int32)[:, None]
    place = ((blocks * N_EXPERT + source_block) * CAP + position).reshape(-1).astype(jnp.int32)
    token_of = (jnp.arange(token_total * TOP, dtype=jnp.int32) // TOP).astype(jnp.int32)
    table = jnp.full((EXPERTS * N_EXPERT * CAP,), token_total, jnp.int32).at[place].set(token_of)
    table = table.reshape(EXPERTS, N_EXPERT * CAP)
    input_pad = jnp.concatenate([inputs, jnp.zeros((1, D), inputs.dtype)], axis=0)
    cot_pad = jnp.concatenate([cotangent, jnp.zeros((1, D), cotangent.dtype)], axis=0)

    def per_expert(pieces):
        return expert_rows(pieces[0], pieces[1], pieces[2], pieces[3], input_pad, cot_pad)
    terms = lax.map(per_expert, (table, w_gate, w_up, w_down))
    per_slot = jnp.take(terms.reshape(-1, D), place, axis=0).reshape(token_total, TOP, D)
    weighted = lax.optimization_barrier(jnp.sum(per_slot * gate_vals[:, :, None].astype(jnp.float32), axis=1))
    return (cotangent.astype(jnp.float32) + weighted).astype(jnp.bfloat16)

def reference(layer_inputs, out_grad, expert_ids, gate_weights, w_gate, w_up, w_down):
    upper = layer_grad(layer_inputs[1], out_grad, expert_ids[1], gate_weights[1], w_gate[1], w_up[1], w_down[1])
    lower = layer_grad(layer_inputs[0], upper, expert_ids[0], gate_weights[0], w_gate[0], w_up[0], w_down[0])
    return jnp.stack([lower, upper])
```

```python
import jax
import jax.numpy as jnp
from jax import lax
from jax.experimental import pallas as pl
from jax.experimental.pallas import tpu as pltpu
from jax.sharding import PartitionSpec as P

AXES = ("section", "expert", "dp")
BF16 = jnp.bfloat16
F32 = jnp.float32
TILE = 256
VMEM_LIMIT = 24 * 1024 * 1024


class Grid:
    def __init__(self):
        self.ny = lax.axis_size("dp")
        experts = lax.axis_size("expert")
        self.nx = self.ny if experts % self.ny == 0 else 1
        self.nz = experts // self.nx
        size = -(-self.nz // 4)
        self.groups = [range(i, min(i + size, self.nz)) for i in range(0, self.nz, size)]

    def pairs(self, secs, dz=0, dx=0, dy=0):
        nz, nx, ny = self.nz, self.nx, self.ny

        def index(s, z, x, y):
            return ((s * nz + z % nz) * nx + x % nx) * ny + y % ny

        return [
            (index(s, z, x, y), index(s, z + dz, x + dx, y + dy))
            for s in secs
            for z in range(nz)
            for x in range(nx)
            for y in range(ny)
        ]

    def send(self, value, secs, **shift):
        return lax.ppermute(value, AXES, self.pairs(secs, **shift))

    def steps(self, group):
        order = [("dx", self.nx), ("dy", self.ny)]
        return order if group % 2 == 0 else order[::-1]

    def gather(self, shard, secs):
        parts = [shard] + [self.send(shard, secs, dz=dz) for dz in range(1, self.nz)]
        out = []
        for group, members in enumerate(self.groups):
            chunk = jnp.concatenate([parts[dz] for dz in members], axis=0)
            for name, count in self.steps(group):
                moved = [self.send(chunk, secs, **{name: k}) for k in range(1, count)]
                chunk = jnp.concatenate([chunk] + moved, axis=0)
            out.append(chunk)
        return out

    def reduce_chunk(self, chunk, group, secs):
        for name, count in self.steps(group)[::-1]:
            rows = chunk.shape[0] // count
            total = chunk[:rows].astype(F32)
            for k in range(1, count):
                part = self.send(chunk[k * rows : (k + 1) * rows], secs, **{name: -k})
                total = total + part.astype(F32)
            chunk = total.astype(BF16)
        members = self.groups[group]
        rows = chunk.shape[0] // len(members)
        found = None
        for i, dz in enumerate(members):
            part = chunk[i * rows : (i + 1) * rows]
            part = (part if dz == 0 else self.send(part, secs, dz=-dz)).astype(F32)
            found = part if found is None else found + part
        return found

    def sources(self):
        expert, y = lax.axis_index("expert"), lax.axis_index("dp")
        z, x = expert // self.nx, expert % self.nx
        found = []
        for group, members in enumerate(self.groups):
            (first, n_first), (second, n_second) = self.steps(group)
            for k2 in range(n_second):
                for k1 in range(n_first):
                    shift = {first: k1, second: k2}
                    sx = (x - shift["dx"] + self.nx) % self.nx
                    sy = (y - shift["dy"] + self.ny) % self.ny
                    for dz in members:
                        sz = (z - dz + self.nz) % self.nz
                        found.append((sz * self.nx + sx) * self.ny + sy)
        return jnp.stack(found).astype(jnp.int32)


def dot(left, right, dims):
    return lax.dot_general(left, right, (dims, ((), ())), preferred_element_type=F32)


def tiles(count):
    return [slice(at, min(at + TILE, count)) for at in range(0, count, TILE)]


def forward_kernel(active, rows, gates, w_gate, w_up, before, out):
    local, _, count, _ = out.shape

    @pl.when(active[0] == 1)
    def _():
        for span in tiles(count):
            for e in range(local):
                pre_gate = dot(rows[span], w_gate[e], ((1,), (1,)))
                pre_up = dot(rows[span], w_up[e], ((1,), (1,)))
                sig = jax.nn.sigmoid(pre_gate)
                weighted = sig * gates[span, e : e + 1]
                slope = pre_up * weighted * (1.0 + pre_gate * (1.0 - sig))
                out[e, 0, span] = slope.astype(BF16)
                out[e, 1, span] = (pre_gate * weighted).astype(BF16)

    @pl.when(active[0] != 1)
    def _():
        out[...] = before[...]


def backward_kernel(active, rows, factors, w_gate, w_up, w_down, out):
    local, _, count, _ = factors.shape

    @pl.when(active[0] == 1)
    def _():
        for span in tiles(count):
            total = None
            for e in range(local):
                hidden = dot(rows[span], w_down[e], ((1,), (1,)))
                gate_grad = (hidden * factors[e, 0, span].astype(F32)).astype(BF16)
                up_grad = (hidden * factors[e, 1, span].astype(F32)).astype(BF16)
                term = dot(gate_grad, w_gate[e], ((1,), (0,))) + dot(up_grad, w_up[e], ((1,), (0,)))
                total = term if total is None else total + term
            out[span] = total.astype(BF16)

    @pl.when(active[0] != 1)
    def _():
        out[...] = jnp.zeros_like(out)


def call_kernel(kernel, name, products, shape, active, *arrays):
    held = pl.BlockSpec(memory_space=pltpu.VMEM)
    weights = next(a for a in arrays if a.ndim == 3)
    moved = 2 * (weights.size * products + sum(a.size for a in arrays if a.ndim != 3))
    return pl.pallas_call(
        kernel,
        out_shape=jax.ShapeDtypeStruct(shape, BF16),
        in_specs=[pl.BlockSpec(memory_space=pltpu.SMEM)] + [held] * len(arrays),
        out_specs=held,
        compiler_params=pltpu.CompilerParams(vmem_limit_bytes=VMEM_LIMIT),
        cost_estimate=pl.CostEstimate(
            flops=2 * weights.size * products * arrays[0].shape[0],
            bytes_accessed=moved,
            transcendentals=0,
        ),
        name=name,
    )(active, *arrays)


def shards(layer_inputs, out_grad, expert_ids, gate_weights, w_gate, w_up, w_down):
    grid = Grid()
    section, y = lax.axis_index("section"), lax.axis_index("dp")
    last = lax.axis_size("section") - 1
    w_gate, w_up = (jnp.swapaxes(w[0], 1, 2) for w in (w_gate, w_up))
    w_down = w_down[0]
    local, width, depth = w_down.shape
    rows = out_grad.shape[0] // grid.ny
    upper, lower = ((section == s).astype(jnp.int32).reshape(1) for s in (last, 0))

    choice = jnp.concatenate([expert_ids[0].astype(F32), gate_weights[0]], axis=1)
    choice = lax.all_gather(choice, "expert", tiled=True)
    ids, vals = jnp.split(choice, 2, axis=1)
    mine = (lax.axis_index("expert") * local + jnp.arange(local, dtype=jnp.int32)).astype(F32)
    table = jnp.sum(jnp.where(ids[:, :, None] == mine, vals[:, :, None], 0.0), axis=1)
    table = table.reshape(-1, rows, local)[grid.sources()]
    gates = table.reshape(len(grid.groups), -1, local)

    def own(value):
        return lax.dynamic_slice_in_dim(value, y * rows, rows, axis=0)

    own_inputs, own_grad = own(layer_inputs[0]), own(out_grad)
    both = grid.gather(jnp.where(section == last, own_inputs, own_grad), (0, 1))
    cots = [lax.ppermute(chunk, "section", [(0, 1)]) for chunk in both]
    def factors_of(active, chunks, before):
        return [
            call_kernel(
                forward_kernel,
                "forward_factors",
                2,
                (local, 2, chunk.shape[0], width),
                active,
                chunk,
                gates[group],
                w_gate,
                w_up,
                before[group],
            )
            for group, chunk in enumerate(chunks)
        ]

    nothing = [jnp.zeros((local, 2, chunk.shape[0], width), BF16) for chunk in both]
    factors = factors_of(upper, both, nothing)
    own_inputs, cots = lax.optimization_barrier((own_inputs, cots))
    factors = factors_of(lower, grid.gather(own_inputs, (0,)), factors)

    def layer(cots, cot_own, sec):
        active = upper if sec == 1 else lower
        total = cot_own.astype(F32)
        for group in range(len(grid.groups)):
            value = call_kernel(
                backward_kernel,
                "backward_rows",
                3,
                cots[group].shape,
                active,
                cots[group],
                factors[group],
                w_gate,
                w_up,
                w_down,
            )
            total = total + grid.reduce_chunk(value, group, (sec,))
        return total.astype(BF16)

    def whole_block(value, sec):
        out = jnp.zeros((rows * grid.ny, value.shape[1]), value.dtype)
        for k in range(grid.ny):
            part = value if k == 0 else grid.send(value, (sec,), dy=k)
            start = (y - k + grid.ny) % grid.ny * rows
            out = lax.dynamic_update_slice_in_dim(out, part, start, axis=0)
        return out

    first = layer(cots, own_grad, 1)
    handed = lax.ppermute(first, "section", [(1, 0)])
    upper_out = whole_block(first, 1)
    second = layer(grid.gather(handed, (0,)), handed, 0)
    lower_out = whole_block(second, 0)
    return jnp.where(section == last, upper_out, lower_out)[None]


def solution(mesh):
    return jax.shard_map(
        shards,
        mesh=mesh,
        in_specs=(
            P("section", "expert", None),
            P("expert", None),
            P("section", "expert", None),
            P("section", "expert", None),
            P("section", "expert", None, "dp"),
            P("section", "expert", None, "dp"),
            P("section", "expert", "dp", None),
        ),
        out_specs=P("section", "expert", None),
        check_vma=False,
    )
```

```python
import functools

import jax
import jax.numpy as jnp
from jax import lax
from jax.experimental import pallas as pl
from jax.experimental.pallas import tpu as pltpu
from jax.sharding import PartitionSpec as P

AXES = ("section", "expert", "dp")
BF16 = jnp.bfloat16
F32 = jnp.float32
TILE = 256
LANES = 128
VMEM_LIMIT = 14 * 1024 * 1024


class Grid:
    def __init__(self):
        self.n = lax.axis_size("dp")
        self.nz = lax.axis_size("expert") // self.n
        size = -(-self.nz // 4)
        self.groups = [range(i, i + size) for i in range(0, self.nz, size)]
        self.half = len(self.groups) // 2

    def send(self, value, shifts):
        n, nz = self.n, self.nz

        def index(s, z, x, y):
            return ((s * nz + z % nz) * n + x % n) * n + y % n

        pairs = []
        for s, shift in shifts.items():
            dz, dx, dy = (shift.get(axis, 0) for axis in "zxy")
            for z in range(nz):
                for x in range(n):
                    for y in range(n):
                        pairs.append((index(s, z, x, y), index(s, z + dz, x + dx, y + dy)))
        return lax.ppermute(value, AXES, pairs)

    def steps(self, sign):
        orders = ("xy", "yx")
        return [
            [{s: {orders[s][step]: sign * k} for s in (0, 1)} for k in range(1, self.n)]
            for step in (0, 1)
        ]

    def spread(self, chunk):
        for shifts in self.steps(1):
            chunk = join([chunk] + [self.send(chunk, shift) for shift in shifts])
        return chunk

    def gather(self, shard):
        parts = [shard]
        for dz in range(1, self.nz):
            parts.append(self.send(parts[-1], {s: {"z": 1} for s in (0, 1)}))
        return [self.spread(join([parts[dz] for dz in members])) for members in self.groups]

    def gather_to(self, sec, shard):
        other = 1 - sec
        out = []
        for j in range(self.half):
            members = zip(self.groups[2 * j], self.groups[2 * j + 1])
            parts = [self.send(shard, {sec: {"z": a}, other: {"z": b}}) for a, b in members]
            chunk = self.spread(join(parts))
            out += [chunk, lax.ppermute(chunk, "section", [(other, sec)])]
        return out

    def reduce_part(self, sec, j, chunk):
        other = 1 - sec
        for shifts in self.steps(-1)[::-1]:
            rows = chunk.shape[0] // self.n
            total = chunk[:rows].astype(F32)
            for k, shift in enumerate(shifts, 1):
                total = total + self.send(chunk[k * rows : (k + 1) * rows], shift).astype(F32)
            chunk = total.astype(BF16)
        rows = chunk.shape[0] // len(self.groups[2 * j])
        found = 0.0
        for i, (a, b) in enumerate(zip(self.groups[2 * j + 1], self.groups[2 * j])):
            part = chunk[i * rows : (i + 1) * rows]
            found = found + self.send(part, {sec: {"z": -a}, other: {"z": -b}}).astype(F32)
        return found


def join(parts):
    return parts[0] if len(parts) == 1 else jnp.concatenate(parts, axis=0)


def dot(left, right, dims):
    return lax.dot_general(left, right, (dims, ((), ())), preferred_element_type=F32)


def tiles(count):
    return [slice(at, min(at + TILE, count)) for at in range(0, count, TILE)]


def parts_of(values):
    found = []
    for _ in range(3):
        rounded = lax.reduce_precision(values, 8, 7)
        found.append(rounded.astype(BF16))
        values = values - rounded
    return found


def forward_kernel(own, top, first, chunk, w_gate, w_up, out, rows, choice):
    local, _, count, _ = out.shape
    depth = rows.shape[1]
    pieces = count // own
    piece = chunk.shape[0] // pieces
    for p in range(pieces):
        source, target = slice(p * piece, p * piece + own), slice(p * own, (p + 1) * own)
        rows[target] = chunk[source, :depth]
        choice[target] = chunk[source, depth:].astype(F32)
    for span in tiles(count):
        table = choice[span]
        ids = table[:, :top]
        weights = sum(table[:, k * top : (k + 1) * top] for k in (1, 2, 3))
        for e in range(local):
            chosen = ids == (first[0] + e).astype(F32)
            gates = jnp.sum(jnp.where(chosen, weights, 0.0), axis=1, keepdims=True)
            pre_gate = dot(rows[span], w_gate[e], ((1,), (1,)))
            pre_up = dot(rows[span], w_up[e], ((1,), (1,)))
            sig = jax.nn.sigmoid(pre_gate)
            weighted = sig * gates
            slope = pre_up * weighted * (1.0 + pre_gate * (1.0 - sig))
            out[e, 0, span] = slope.astype(BF16)
            out[e, 1, span] = (pre_gate * weighted).astype(BF16)


def turned(n, unit, units):
    members = units // (n * n)
    place, member = divmod(unit, members)
    return (place % n * n + place // n) * members + member


def backward_kernel(layout, active, *refs):
    n, own, turn_in, turn_out = layout
    mixed = len(refs) == 9
    chunk, far = refs[0], refs[1] if mixed else None
    factors, w_gate, w_up, w_down, other, out, rows = refs[1 + mixed :]
    local, _, count, _ = factors.shape
    units = count // own

    @pl.when(active[0] == 1)
    def _():
        for u in range(units):
            at, from_unit = u * own, turned(n, u, units)
            if mixed:
                piece, part = chunk.shape[0] // units, far.shape[0] // units
                rows[at : at + own - part] = chunk[u * piece + own : (u + 1) * piece, : rows.shape[1]]
                rows[at + own - part : at + own] = far[from_unit * part : (from_unit + 1) * part]
            else:
                start = (from_unit if turn_in else u) * own
                rows[at : at + own] = chunk[start : start + own]
        for span in tiles(count):
            total = None
            for e in range(local):
                hidden = dot(rows[span], w_down[e], ((1,), (1,)))
                gate_grad = (hidden * factors[e, 0, span].astype(F32)).astype(BF16)
                up_grad = (hidden * factors[e, 1, span].astype(F32)).astype(BF16)
                term = dot(gate_grad, w_gate[e], ((1,), (0,))) + dot(up_grad, w_up[e], ((1,), (0,)))
                total = term if total is None else total + term
            total = total.astype(BF16)
            for at in range(span.start, span.stop, own):
                unit = at // own
                start = (turned(n, unit, units) if turn_out else unit) * own
                out[start : start + own] = total[at - span.start : at - span.start + own]

    @pl.when(active[0] != 1)
    def _():
        out[...] = other[...]


def call_kernel(kernel, name, terms, shape, scratch, scalar, *arrays):
    held = pl.BlockSpec(memory_space=pltpu.VMEM)
    weights = [a for a in arrays if a.ndim == 3]
    count = shape[-2]
    return pl.pallas_call(
        kernel,
        out_shape=jax.ShapeDtypeStruct(shape, BF16),
        in_specs=[pl.BlockSpec(memory_space=pltpu.SMEM)] + [held] * len(arrays),
        out_specs=held,
        scratch_shapes=scratch,
        compiler_params=pltpu.CompilerParams(vmem_limit_bytes=VMEM_LIMIT),
        cost_estimate=pl.CostEstimate(
            flops=2 * weights[0].size * terms * count,
            bytes_accessed=sum(2 * a.size for a in arrays),
            transcendentals=0,
        ),
        name=name,
    )(scalar, *arrays)


def shards(layer_inputs, out_grad, expert_ids, gate_weights, w_gate, w_up, w_down):
    grid = Grid()
    section, y = lax.axis_index("section"), lax.axis_index("dp")
    w_gate, w_up = (jnp.swapaxes(w[0], 1, 2) for w in (w_gate, w_up))
    w_down = w_down[0]
    local, width, depth = w_down.shape
    rows = out_grad.shape[0] // grid.n
    part = rows // 2
    is_section = [(section == s).astype(jnp.int32).reshape(1) for s in (0, 1)]
    first_expert = (lax.axis_index("expert") * local).astype(jnp.int32).reshape(1)

    def own(value):
        return lax.dynamic_slice_in_dim(value, y * rows, rows)

    own_grad = own(out_grad)
    top = expert_ids.shape[2]
    choice = [own(expert_ids[0]).astype(BF16)] + parts_of(own(gate_weights[0]))
    choice.append(jnp.zeros((rows, LANES - 4 * top), BF16))
    own_rows = jnp.concatenate([own(layer_inputs[0])] + choice, axis=1)
    half_grad = lax.dynamic_slice_in_dim(out_grad, y * rows + (1 - section) * part, part)
    half_grad = jnp.pad(half_grad, ((0, 0), (0, LANES)))
    chunks = grid.gather(jnp.concatenate([own_rows, half_grad], axis=0))
    piece = rows + part
    count = chunks[0].shape[0] // piece * rows
    factors, far = [], []
    for chunk in chunks:
        factors.append(
            call_kernel(
                functools.partial(forward_kernel, rows, top),
                "forward_factors",
                2,
                (local, 2, count, width),
                [pltpu.VMEM((count, depth), BF16), pltpu.VMEM((count, LANES), F32)],
                first_expert,
                chunk,
                w_gate,
                w_up,
            )
        )
        behind = chunk.reshape(-1, piece, depth + LANES)[:, rows:, :depth].reshape(-1, depth)
        far.append(lax.ppermute(behind, "section", [(0, 1)]))

    def rows_of(sec, group, cot_rows, other):
        odd = group % 2 == 1
        return call_kernel(
            functools.partial(backward_kernel, (grid.n, rows, odd, not odd)),
            "backward_rows",
            3,
            (count, depth),
            [pltpu.VMEM((count, depth), BF16)],
            is_section[sec],
            *cot_rows,
            factors[group],
            w_gate,
            w_up,
            w_down,
            other,
        )

    def layer(sec, cots, cotangent):
        nothing = jnp.zeros((count, depth), BF16)
        found = 0.0
        for j in range(grid.half):
            even = rows_of(sec, 2 * j, cots[2 * j], nothing)
            handed = lax.ppermute(even, "section", [(sec, 1 - sec)])
            odd = rows_of(sec, 2 * j + 1, cots[2 * j + 1], handed)
            found = found + grid.reduce_part(sec, j, odd)
        found = found + lax.ppermute(found, "section", [(0, 1), (1, 0)])
        return (cotangent.astype(F32) + found).astype(BF16)

    def whole_block(value, sec):
        parts = [value] + [grid.send(value, {sec: {"y": k}}) for k in range(1, grid.n)]
        stacked = jnp.stack(parts)
        return jnp.concatenate([stacked[(y - i + grid.n) % grid.n] for i in range(grid.n)], axis=0)

    first = layer(1, list(zip(chunks, far)), own_grad)
    cots = [(chunk,) for chunk in grid.gather_to(0, first)]
    upper_out = whole_block(first, 1)
    second = layer(0, cots, first)
    lower_out = whole_block(second, 0)
    return jnp.where(section == 1, upper_out, lower_out)[None]


def solution(mesh):
    return jax.shard_map(
        shards,
        mesh=mesh,
        in_specs=(
            P("section", "expert", None),
            P("expert", None),
            P("section", "expert", None),
            P("section", "expert", None),
            P("section", "expert", None, "dp"),
            P("section", "expert", None, "dp"),
            P("section", "expert", "dp", None),
        ),
        out_specs=P("section", "expert", None),
        check_vma=False,
    )
```

```python
import functools

import jax
import jax.numpy as jnp
from jax import lax
from jax.experimental import pallas as pl
from jax.experimental.pallas import tpu as pltpu
from jax.sharding import PartitionSpec as P

AXES = ("section", "expert", "dp")
BF16 = jnp.bfloat16
F32 = jnp.float32
TILE = 256
LANES = 128
VMEM_LIMIT = 14 * 1024 * 1024


class Grid:
    def __init__(self):
        self.n = lax.axis_size("dp")
        self.nz = lax.axis_size("expert") // self.n
        size = -(-self.nz // 4)
        self.groups = [range(i, i + size) for i in range(0, self.nz, size)]
        self.half = len(self.groups) // 2

    def send(self, value, shifts):
        n, nz = self.n, self.nz

        def index(s, z, x, y):
            return ((s * nz + z % nz) * n + x % n) * n + y % n

        pairs = []
        for s, shift in shifts.items():
            dz, dx, dy, ds = (shift.get(axis, 0) for axis in "zxys")
            for z in range(nz):
                for x in range(n):
                    for y in range(n):
                        pairs.append((index(s, z, x, y), index((s + ds) % 2, z + dz, x + dx, y + dy)))
        return lax.ppermute(value, AXES, pairs)

    def steps(self, sign):
        orders = ("xy", "yx")
        return [
            [{s: {orders[s][step]: sign * k} for s in (0, 1)} for k in range(1, self.n)]
            for step in (0, 1)
        ]

    def step(self, step, chunk):
        return join([chunk] + [self.send(chunk, shift) for shift in self.steps(1)[step]])

    def members(self, j):
        return list(zip(self.groups[2 * j], self.groups[2 * j + 1]))

    def along_z(self, shard, j):
        return join([self.send(shard, {0: {"z": a}, 1: {"z": b}}) for a, b in self.members(j)])

    def reduce_part(self, j, chunk):
        for shifts in self.steps(-1)[::-1]:
            rows = chunk.shape[0] // self.n
            total = chunk[:rows].astype(F32)
            for k, shift in enumerate(shifts, 1):
                total = total + self.send(chunk[k * rows : (k + 1) * rows], shift).astype(F32)
            chunk = total.astype(BF16)
        members = self.members(j)
        rows = chunk.shape[0] // len(members)
        found = 0.0
        for i, (a, b) in enumerate(members):
            part = chunk[i * rows : (i + 1) * rows]
            found = found + self.send(part, {0: {"z": -a}, 1: {"z": -b}}).astype(F32)
        return found


def after(kept, value, *others):
    tokens = [t[(0,) * (t.ndim - 2)][:16, :128] for t in jax.tree.leaves(others)]
    value, tokens = lax.optimization_barrier((value, tokens))
    kept.extend(tokens)
    return value


def join(parts):
    return parts[0] if len(parts) == 1 else jnp.concatenate(parts, axis=0)


def dot(left, right, dims):
    return lax.dot_general(left, right, (dims, ((), ())), preferred_element_type=F32)


def tiles(count):
    return [slice(at, min(at + TILE, count)) for at in range(0, count, TILE)]


def parts_of(values):
    found = []
    for _ in range(3):
        rounded = lax.reduce_precision(values, 8, 7)
        found.append(rounded.astype(BF16))
        values = values - rounded
    return found


def forward_kernel(own, top, first, chunk, w_gate, w_up, out, rows, choice):
    local, _, count, _ = out.shape
    depth = rows.shape[1]
    pieces = count // own
    piece = chunk.shape[0] // pieces
    for p in range(pieces):
        source, target = slice(p * piece, p * piece + own), slice(p * own, (p + 1) * own)
        rows[target] = chunk[source, :depth]
        choice[target] = chunk[source, depth:].astype(F32)
    for span in tiles(count):
        table = choice[span]
        ids = table[:, :top]
        weights = sum(table[:, k * top : (k + 1) * top] for k in (1, 2, 3))
        for e in range(local):
            chosen = ids == (first[0] + e).astype(F32)
            gates = jnp.sum(jnp.where(chosen, weights, 0.0), axis=1, keepdims=True)
            pre_gate = dot(rows[span], w_gate[e], ((1,), (1,)))
            pre_up = dot(rows[span], w_up[e], ((1,), (1,)))
            sig = jax.nn.sigmoid(pre_gate)
            weighted = sig * gates
            slope = pre_up * weighted * (1.0 + pre_gate * (1.0 - sig))
            out[e, 0, span] = slope.astype(BF16)
            out[e, 1, span] = (pre_gate * weighted).astype(BF16)


def backward_kernel(own, behind, chunk, factors, w_gate, w_up, w_down, *rest):
    out, rows = rest[-2:]
    local, _, count, _ = factors.shape
    units = count // own
    piece = chunk.shape[0] // units
    for u in range(units):
        at = u * piece + behind
        rows[u * own : (u + 1) * own] = chunk[at : at + own, : rows.shape[1]]
    for span in tiles(count):
        total = None
        for e in range(local):
            hidden = dot(rows[span], w_down[e], ((1,), (1,)))
            gate_grad = (hidden * factors[e, 0, span].astype(F32)).astype(BF16)
            up_grad = (hidden * factors[e, 1, span].astype(F32)).astype(BF16)
            term = dot(gate_grad, w_gate[e], ((1,), (0,))) + dot(up_grad, w_up[e], ((1,), (0,)))
            total = term if total is None else total + term
        out[span] = total.astype(BF16)


def load_kernel(mine, own, other, out, sems):
    def load(source):
        copies = [
            pltpu.make_async_copy(source.at[e], out.at[e], sems.at[e]) for e in range(out.shape[0])
        ]
        for copy in copies:
            copy.start()
        for copy in copies:
            copy.wait()

    @pl.when(mine[0] == 1)
    def _():
        load(own)

    @pl.when(mine[0] != 1)
    def _():
        load(other)


def load_weights(mine, own, other):
    anywhere = pl.BlockSpec(memory_space=pl.ANY)
    return pl.pallas_call(
        load_kernel,
        out_shape=jax.ShapeDtypeStruct(own.shape, own.dtype),
        in_specs=[pl.BlockSpec(memory_space=pltpu.SMEM), anywhere, anywhere],
        out_specs=pl.BlockSpec(memory_space=pltpu.VMEM),
        scratch_shapes=[pltpu.SemaphoreType.DMA((own.shape[0],))],
        compiler_params=pltpu.CompilerParams(vmem_limit_bytes=VMEM_LIMIT),
        cost_estimate=pl.CostEstimate(flops=0, bytes_accessed=2 * own.size * 2, transcendentals=0),
        name="load_weights",
    )(mine, own, other)


def call_kernel(kernel, name, terms, shape, scratch, scalars, *arrays, extra=()):
    held = pl.BlockSpec(memory_space=pltpu.VMEM)
    weights = [a for a in arrays if a.ndim == 3]
    count = shape[-2]
    return pl.pallas_call(
        kernel,
        out_shape=jax.ShapeDtypeStruct(shape, BF16),
        in_specs=[pl.BlockSpec(memory_space=pltpu.SMEM)] * len(scalars) + [held] * len(arrays)
        + [pl.BlockSpec(memory_space=pl.ANY)] * len(extra),
        out_specs=held,
        scratch_shapes=scratch,
        compiler_params=pltpu.CompilerParams(vmem_limit_bytes=VMEM_LIMIT),
        cost_estimate=pl.CostEstimate(
            flops=2 * weights[0].size * terms * count,
            bytes_accessed=sum(2 * a.size for a in arrays),
            transcendentals=0,
        ),
        name=name,
    )(*scalars, *arrays, *extra)


def shards(layer_inputs, out_grad, expert_ids, gate_weights, w_gate, w_up, w_down):
    grid = Grid()
    kept = []
    section, y = lax.axis_index("section"), lax.axis_index("dp")
    w_gate, w_up = (jnp.swapaxes(w[0], 1, 2) for w in (w_gate, w_up))
    w_down = w_down[0]
    weights = (w_gate, w_up, w_down)
    local, width, depth = w_down.shape
    rows = out_grad.shape[0] // grid.n
    top = expert_ids.shape[2]
    swap = [(0, 1), (1, 0)]
    first_expert = (lax.axis_index("expert") * local).astype(jnp.int32).reshape(1)

    def own(value):
        return lax.dynamic_slice_in_dim(value, y * rows, rows)

    own_grad = own(out_grad)
    choice = [own(expert_ids[0]).astype(BF16)] + parts_of(own(gate_weights[0]))
    choice.append(jnp.zeros((rows, LANES - 4 * top), BF16))
    mine = jnp.concatenate([own(layer_inputs[0])] + choice, axis=1)
    theirs = lax.ppermute(mine, "section", swap)
    upper_rows = jnp.where(section == 1, mine, theirs)
    lower_rows = jnp.where(section == 1, theirs, mine)
    weights = list(weights)
    late = after(kept, weights, theirs)
    others = [lax.ppermute(w, "section", swap) for w in late]

    def held_weight(layer, i, after_value):
        is_mine = after(kept, (section == layer).astype(jnp.int32).reshape(1), after_value)
        return load_weights(is_mine, weights[i], others[i])

    def forward(chunk, held):
        count = chunk_rows
        return call_kernel(
            functools.partial(forward_kernel, rows, top),
            "forward_factors",
            2,
            (local, 2, count, width),
            [pltpu.VMEM((count, depth), BF16), pltpu.VMEM((count, LANES), F32)],
            (first_expert,),
            chunk,
            *held[:2],
        )

    def backward(chunk, behind, factors, held, extra=()):
        count = chunk_rows
        return call_kernel(
            functools.partial(backward_kernel, rows, behind),
            "backward_rows",
            3,
            (count, depth),
            [pltpu.VMEM((count, depth), BF16)],
            (),
            chunk,
            factors,
            *held,
            extra=extra,
        )

    def reduce(products, cotangent):
        found = 0.0
        for j, product in enumerate(products):
            found = found + grid.reduce_part(j, product)
        found = found + lax.ppermute(found, "section", swap)
        return (cotangent.astype(F32) + found).astype(BF16)

    padded_grad = jnp.pad(own_grad, ((0, 0), (0, LANES)))
    shard = jnp.concatenate([upper_rows, padded_grad], axis=0)
    half0 = grid.step(0, grid.along_z(shard, 0))
    chunk0 = grid.step(1, half0)
    chunk_rows = chunk0.shape[0] // 2
    z1 = grid.along_z(after(kept, shard, half0), 1)
    half1 = grid.step(0, z1)
    held = [held_weight(1, i, upper_rows) for i in range(3)]
    chunk1 = grid.step(1, after(kept, half1, chunk0, held))
    factors = forward(chunk0, held)

    lower_rows = after(kept, lower_rows, z1)
    low_half0 = grid.step(0, after(kept, grid.along_z(lower_rows, 0), half1))
    low0 = grid.step(1, after(kept, low_half0, chunk1))
    low_z1 = grid.along_z(after(kept, lower_rows, low_half0), 1)
    low_half1 = grid.step(0, low_z1)
    low1 = grid.step(1, after(kept, low_half1, low0))

    product0 = backward(chunk0, rows, factors, held)
    factors = forward(after(kept, chunk1, low_half0, product0), held)
    product1 = backward(chunk1, rows, after(kept, factors, low_half1), held)
    products = [product0, product1]
    held = [held_weight(0, i, product0) for i in range(3)]
    factors = [forward(chunk, held) for chunk in (low0, low1)]

    first = reduce(products, own_grad)
    z0 = grid.along_z(first, 0)
    half0 = grid.step(0, z0)
    z1 = grid.along_z(after(kept, first, z0), 1)
    half1 = grid.step(0, after(kept, z1, half0, factors))
    chunk0 = grid.step(1, half0)
    chunk1 = grid.step(1, after(kept, half1, chunk0))
    cots = [chunk0, chunk1]
    products = [
        backward(cots[0], 0, factors[0], held),
        backward(cots[1], 0, factors[1], held, kept),
    ]
    second = reduce(products, first)

    def whole_block(value, sec):
        parts = [value] + [grid.send(value, {sec: {"y": k}}) for k in range(1, grid.n)]
        stacked = jnp.stack(parts)
        return jnp.concatenate([stacked[(y - i + grid.n) % grid.n] for i in range(grid.n)], axis=0)

    upper_out = whole_block(first, 1)
    lower_out = whole_block(second, 0)
    return jnp.where(section == 1, upper_out, lower_out)[None]


def solution(mesh):
    return jax.shard_map(
        shards,
        mesh=mesh,
        in_specs=(
            P("section", "expert", None),
            P("expert", None),
            P("section", "expert", None),
            P("section", "expert", None),
            P("section", "expert", None, "dp"),
            P("section", "expert", None, "dp"),
            P("section", "expert", "dp", None),
        ),
        out_specs=P("section", "expert", None),
        check_vma=False,
    )
```

```python
import functools

import jax
import jax.numpy as jnp
from jax import lax
from jax.experimental import pallas as pl
from jax.experimental.pallas import tpu as pltpu
from jax.sharding import PartitionSpec as P

AXES = ("section", "expert", "dp")
BF16 = jnp.bfloat16
F32 = jnp.float32
TILE = 256
LANES = 128
VMEM_LIMIT = 14 * 1024 * 1024


class Grid:
    def __init__(self):
        self.n = lax.axis_size("dp")
        self.nz = lax.axis_size("expert") // self.n
        size = -(-self.nz // 4)
        self.groups = [range(i, i + size) for i in range(0, self.nz, size)]
        self.half = len(self.groups) // 2

    def send(self, value, shifts):
        n, nz = self.n, self.nz

        def index(s, z, x, y):
            return ((s * nz + z % nz) * n + x % n) * n + y % n

        pairs = []
        for s, shift in shifts.items():
            dz, dx, dy, ds = (shift.get(axis, 0) for axis in "zxys")
            for z in range(nz):
                for x in range(n):
                    for y in range(n):
                        pairs.append((index(s, z, x, y), index((s + ds) % 2, z + dz, x + dx, y + dy)))
        return lax.ppermute(value, AXES, pairs)

    def steps(self, sign):
        orders = ("xy", "yx")
        return [
            [{s: {orders[s][step]: sign * k} for s in (0, 1)} for k in range(1, self.n)]
            for step in (0, 1)
        ]

    def step(self, step, chunk):
        return join([chunk] + [self.send(chunk, shift) for shift in self.steps(1)[step]])

    def members(self, j):
        return list(zip(self.groups[2 * j], self.groups[2 * j + 1]))

    def along_z(self, shard, j):
        return join([self.send(shard, {0: {"z": a}, 1: {"z": b}}) for a, b in self.members(j)])

    def reduce_part(self, j, chunk):
        for shifts in self.steps(-1)[::-1]:
            rows = chunk.shape[0] // self.n
            total = chunk[:rows].astype(F32)
            for k, shift in enumerate(shifts, 1):
                total = total + self.send(chunk[k * rows : (k + 1) * rows], shift).astype(F32)
            chunk = total.astype(BF16)
        members = self.members(j)
        rows = chunk.shape[0] // len(members)
        found = 0.0
        for i, (a, b) in enumerate(members):
            part = chunk[i * rows : (i + 1) * rows]
            found = found + self.send(part, {0: {"z": -a}, 1: {"z": -b}}).astype(F32)
        return found


def after(kept, value, *others):
    tokens = [t[(0,) * (t.ndim - 2)][:16, :128] for t in jax.tree.leaves(others)]
    value, tokens = lax.optimization_barrier((value, tokens))
    kept.extend(tokens)
    return value


def join(parts):
    return parts[0] if len(parts) == 1 else jnp.concatenate(parts, axis=0)


def dot(left, right, dims):
    return lax.dot_general(left, right, (dims, ((), ())), preferred_element_type=F32)


def tiles(count):
    return [slice(at, min(at + TILE, count)) for at in range(0, count, TILE)]


def parts_of(values):
    found = []
    for _ in range(3):
        rounded = lax.reduce_precision(values, 8, 7)
        found.append(rounded.astype(BF16))
        values = values - rounded
    return found


def forward_kernel(own, top, first, chunk, w_gate, w_up, out, rows, choice):
    local, _, count, _ = out.shape
    depth = rows.shape[1]
    pieces = count // own
    piece = chunk.shape[0] // pieces
    for p in range(pieces):
        source, target = slice(p * piece, p * piece + own), slice(p * own, (p + 1) * own)
        rows[target] = chunk[source, :depth]
        choice[target] = chunk[source, depth:].astype(F32)
    for span in tiles(count):
        table = choice[span]
        ids = table[:, :top]
        weights = sum(table[:, k * top : (k + 1) * top] for k in (1, 2, 3))
        for e in range(local):
            chosen = ids == (first[0] + e).astype(F32)
            gates = jnp.sum(jnp.where(chosen, weights, 0.0), axis=1, keepdims=True)
            pre_gate = dot(rows[span], w_gate[e], ((1,), (1,)))
            pre_up = dot(rows[span], w_up[e], ((1,), (1,)))
            sig = jax.nn.sigmoid(pre_gate)
            weighted = sig * gates
            slope = pre_up * weighted * (1.0 + pre_gate * (1.0 - sig))
            out[e, 0, span] = slope.astype(BF16)
            out[e, 1, span] = (pre_gate * weighted).astype(BF16)


def backward_kernel(own, behind, chunk, factors, w_gate, w_up, w_down, *rest):
    out, rows = rest[-2:]
    local, _, count, _ = factors.shape
    units = count // own
    piece = chunk.shape[0] // units
    for u in range(units):
        at = u * piece + behind
        rows[u * own : (u + 1) * own] = chunk[at : at + own, : rows.shape[1]]
    for span in tiles(count):
        total = None
        for e in range(local):
            hidden = dot(rows[span], w_down[e], ((1,), (1,)))
            gate_grad = (hidden * factors[e, 0, span].astype(F32)).astype(BF16)
            up_grad = (hidden * factors[e, 1, span].astype(F32)).astype(BF16)
            term = dot(gate_grad, w_gate[e], ((1,), (0,))) + dot(up_grad, w_up[e], ((1,), (0,)))
            total = term if total is None else total + term
        out[span] = total.astype(BF16)


def load_kernel(mine, own, other, out, sems):
    def load(source):
        copies = [
            pltpu.make_async_copy(source.at[e], out.at[e], sems.at[e]) for e in range(out.shape[0])
        ]
        for copy in copies:
            copy.start()
        for copy in copies:
            copy.wait()

    @pl.when(mine[0] == 1)
    def _():
        load(own)

    @pl.when(mine[0] != 1)
    def _():
        load(other)


def load_weights(mine, own, other):
    anywhere = pl.BlockSpec(memory_space=pl.ANY)
    return pl.pallas_call(
        load_kernel,
        out_shape=jax.ShapeDtypeStruct(own.shape, own.dtype),
        in_specs=[pl.BlockSpec(memory_space=pltpu.SMEM), anywhere, anywhere],
        out_specs=pl.BlockSpec(memory_space=pltpu.VMEM),
        scratch_shapes=[pltpu.SemaphoreType.DMA((own.shape[0],))],
        compiler_params=pltpu.CompilerParams(vmem_limit_bytes=VMEM_LIMIT),
        cost_estimate=pl.CostEstimate(flops=0, bytes_accessed=2 * own.size * 2, transcendentals=0),
        name="load_weights",
    )(mine, own, other)


def call_kernel(kernel, name, terms, shape, scratch, scalars, *arrays, extra=()):
    held = pl.BlockSpec(memory_space=pltpu.VMEM)
    weights = [a for a in arrays if a.ndim == 3]
    count = shape[-2]
    return pl.pallas_call(
        kernel,
        out_shape=jax.ShapeDtypeStruct(shape, BF16),
        in_specs=[pl.BlockSpec(memory_space=pltpu.SMEM)] * len(scalars) + [held] * len(arrays)
        + [pl.BlockSpec(memory_space=pl.ANY)] * len(extra),
        out_specs=held,
        scratch_shapes=scratch,
        compiler_params=pltpu.CompilerParams(vmem_limit_bytes=VMEM_LIMIT),
        cost_estimate=pl.CostEstimate(
            flops=2 * weights[0].size * terms * count,
            bytes_accessed=sum(2 * a.size for a in arrays),
            transcendentals=0,
        ),
        name=name,
    )(*scalars, *arrays, *extra)


def shards(layer_inputs, out_grad, expert_ids, gate_weights, w_gate, w_up, w_down):
    grid = Grid()
    kept = []
    section, y = lax.axis_index("section"), lax.axis_index("dp")
    w_gate, w_up = (jnp.swapaxes(w[0], 1, 2) for w in (w_gate, w_up))
    w_down = w_down[0]
    weights = (w_gate, w_up, w_down)
    local, width, depth = w_down.shape
    rows = out_grad.shape[0] // grid.n
    top = expert_ids.shape[2]
    swap = [(0, 1), (1, 0)]
    first_expert = (lax.axis_index("expert") * local).astype(jnp.int32).reshape(1)

    def own(value):
        return lax.dynamic_slice_in_dim(value, y * rows, rows)

    own_grad = own(out_grad)
    choice = [own(expert_ids[0]).astype(BF16)] + parts_of(own(gate_weights[0]))
    choice.append(jnp.zeros((rows, LANES - 4 * top), BF16))
    mine = jnp.concatenate([own(layer_inputs[0])] + choice, axis=1)
    theirs = lax.ppermute(mine, "section", swap)
    upper_rows = jnp.where(section == 1, mine, theirs)
    lower_rows = jnp.where(section == 1, theirs, mine)
    weights = list(weights)
    late = after(kept, weights, theirs)
    others = [lax.ppermute(w, "section", swap) for w in late]

    def held_weight(layer, i, after_value):
        is_mine = after(kept, (section == layer).astype(jnp.int32).reshape(1), after_value)
        return load_weights(is_mine, weights[i], others[i])

    def forward(chunk, held):
        count = chunk_rows
        return call_kernel(
            functools.partial(forward_kernel, rows, top),
            "forward_factors",
            2,
            (local, 2, count, width),
            [pltpu.VMEM((count, depth), BF16), pltpu.VMEM((count, LANES), F32)],
            (first_expert,),
            chunk,
            *held[:2],
        )

    def backward(chunk, behind, factors, held, extra=()):
        count = chunk_rows
        return call_kernel(
            functools.partial(backward_kernel, rows, behind),
            "backward_rows",
            3,
            (count, depth),
            [pltpu.VMEM((count, depth), BF16)],
            (),
            chunk,
            factors,
            *held,
            extra=extra,
        )

    def reduce(products, cotangent):
        found = 0.0
        for j, product in enumerate(products):
            found = found + grid.reduce_part(j, product)
        found = found + lax.ppermute(found, "section", swap)
        return (cotangent.astype(F32) + found).astype(BF16)

    padded_grad = jnp.pad(own_grad, ((0, 0), (0, LANES)))
    shard = jnp.concatenate([upper_rows, padded_grad], axis=0)
    half0 = grid.step(0, grid.along_z(shard, 0))
    chunk0 = grid.step(1, half0)
    chunk_rows = chunk0.shape[0] // 2
    z1 = grid.along_z(after(kept, shard, half0), 1)
    half1 = grid.step(0, z1)
    held = [held_weight(1, i, upper_rows) for i in range(3)]
    chunk1 = grid.step(1, after(kept, half1, chunk0, held))
    factors = forward(chunk0, held)

    lower_rows = after(kept, lower_rows, z1)
    low_half0 = grid.step(0, after(kept, grid.along_z(lower_rows, 0), half1))
    low0 = grid.step(1, after(kept, low_half0, chunk1))
    low_z1 = grid.along_z(after(kept, lower_rows, low_half0), 1)
    low_half1 = grid.step(0, low_z1)
    low1 = grid.step(1, after(kept, low_half1, low0))

    product0 = backward(chunk0, rows, factors, held)
    factors = forward(after(kept, chunk1, product0), held)
    product1 = backward(chunk1, rows, factors, held)
    products = [product0, product1]
    held = [held_weight(0, i, product0) for i in range(3)]
    factors = [forward(chunk, held) for chunk in (low0, low1)]

    first = reduce(products, own_grad)
    z0 = grid.along_z(first, 0)
    half0 = grid.step(0, z0)
    z1 = grid.along_z(after(kept, first, z0), 1)
    half1 = grid.step(0, after(kept, z1, half0, factors))
    chunk0 = grid.step(1, half0)
    chunk1 = grid.step(1, after(kept, half1, chunk0))
    cots = [chunk0, chunk1]
    products = [
        backward(cots[0], 0, factors[0], held),
        backward(cots[1], 0, factors[1], held, kept),
    ]
    second = reduce(products, first)

    def whole_block(value, sec):
        parts = [value] + [grid.send(value, {sec: {"y": k}}) for k in range(1, grid.n)]
        stacked = jnp.stack(parts)
        return jnp.concatenate([stacked[(y - i + grid.n) % grid.n] for i in range(grid.n)], axis=0)

    upper_out = whole_block(first, 1)
    lower_out = whole_block(second, 0)
    return jnp.where(section == 1, upper_out, lower_out)[None]


def solution(mesh):
    return jax.shard_map(
        shards,
        mesh=mesh,
        in_specs=(
            P("section", "expert", None),
            P("expert", None),
            P("section", "expert", None),
            P("section", "expert", None),
            P("section", "expert", None, "dp"),
            P("section", "expert", None, "dp"),
            P("section", "expert", "dp", None),
        ),
        out_specs=P("section", "expert", None),
        check_vma=False,
    )
```
